32 devices in a mesh: win: 8 (over z, y), space: 4 (over x, core).
Axes of the slice: x: 2, y: 2, z: 4, core: 2. Of those that a mesh axis runs over, the one named last changes fastest.
Arguments:
- increment: float32 [8, 64, 256, 256], P('win', 'space'), may hold values from -6 to 6
- multiplier: float32 [8, 64, 256, 256], P('win', 'space'), may hold values from -6 to 6
- obs_dual: float32 [8, 4096], P('win', 'space'), may hold values from -6 to 6
- obs_sites: int32 [8, 3, 4096], P('win'), may hold values from 0 to 255, as said below
- obs_variance: float32 [8, 4096], P('win', 'space'), may hold values from 0.5 to 2
- trajectory: bfloat16 [8, 64, 256, 256], P('win', None, 'space'), may hold values from -6 to 6
- diffusion: float32 [64], replicated, may hold values from 0.05 to 0.2
- drift_rows: float32 [64], replicated, may hold values from -0.25 to 0.25
- drift_cols: float32 [64], replicated, may hold values from -0.25 to 0.25
- spread: float32 [64], replicated, may hold values from 0.5 to 2
- row_factor: float32 [256, 256], replicated, may hold values from -0.375 to 0.375
- col_factor: float32 [256, 256], replicated, may hold values from -0.375 to 0.375
- layer_in: bfloat16 [1024, 64], replicated, may hold values from -0.75 to 0.75
- bias_in: float32 [1024], replicated, may hold values from -4 to 4
- layer_out: bfloat16 [64, 1024], replicated, may hold values from -0.1875 to 0.1875
Outputs:
- state_out: float32 [8, 64, 256, 256], P('win', 'space')
- obs_out: float32 [8, 4096], P('win', 'space')
- mult_out: float32 [8, 64, 256, 256], P('win', 'space')
The draws below stay inside these ranges and needn't reach their ends.
Inputs may be any that keep to these rules, and one draw needn't show every extreme that they name: `obs_sites`: row 0 holds a level below 64, row 1 a first index below 256, row 2 a second index below 256; positions may repeat.
All inputs are finite; a program needn't handle non-finite values.
Results may differ from the reference program's by a relative error of at most 0.0011.
Values sent between devices are 32-bit elements; how exact they have to be, the bound alone decides.
No kernel may reach another device: no remote copies, remote signals or barrier semaphores. Data moves between devices by JAX's collectives and lax.ppermute only.
A program may use at most 128 MiB of HBM per device.

```python
import math
import jax
import jax.numpy as jnp
from jax import lax

NX = 256
NY = 256
LEV = 64
HID = 1024
STEPS = 4
SUBWINS = 8
NOBS = 4096


def draw_obs_sites(key, part):
    keys = jax.random.split(jax.random.fold_in(key, 7), 3)
    levels = jax.random.randint(keys[0], (SUBWINS, NOBS), 0, LEV)
    first = jax.random.randint(keys[1], (SUBWINS, NOBS), 0, NX)
    second = jax.random.randint(keys[2], (SUBWINS, NOBS), 0, NY)
    levels = levels.at[:, 0].set(LEV - 1).at[:, 1].set(0)
    first = first.at[:, 0].set(NX - 1).at[:, 1].set(0)
    second = second.at[:, 0].set(NY - 1).at[:, 1].set(0)
    return jnp.stack([levels, first, second], 1).astype(jnp.int32)


def block_levels(key, extent, cuts, low, top_value):
    gain, own = 1.0, jax.random.fold_in(key, 6)
    for axis_at, blocks in cuts:
        heights = jnp.exp(jax.random.uniform(jax.random.fold_in(own, axis_at), (blocks,), jnp.float32, low / len(cuts), top_value / len(cuts)))
        gain = gain * jnp.repeat(heights, extent[axis_at] // blocks).reshape([-1 if axis == axis_at else 1 for axis in range(len(extent))])
    return gain


def bell_draw(rng, shape, width, most, shards=(), held_as=jnp.bfloat16):
    level = block_levels(rng, shape, shards, -0.22, 0.18) if shards else 1.0
    result = jax.random.normal(rng, shape, jnp.float32) * width * level
    return jnp.minimum(jnp.maximum(result, -most), most).astype(held_as)


def setup_inputs(seed: int = 0) -> dict:
    key_list = jax.random.split(jax.random.key(seed), 16)
    return {
        "increment": bell_draw(key_list[0], (SUBWINS, LEV, NX, NY), 1.0, 6.0, ((0, 8), (1, 4)), jnp.float32),
        "multiplier": bell_draw(key_list[1], (SUBWINS, LEV, NX, NY), 1.0, 6.0, ((0, 8), (1, 4)), jnp.float32),
        "obs_dual": bell_draw(key_list[2], (SUBWINS, NOBS), 1.0, 6.0, ((0, 8), (1, 4)), jnp.float32),
        "obs_sites": draw_obs_sites(jax.random.fold_in(key_list[15], 71), 0),
        "obs_variance": jnp.clip(jnp.exp(math.log(2.0) - 1.3862944 * jax.random.uniform(key_list[4], (SUBWINS, NOBS), jnp.float32) ** block_levels(key_list[4], (SUBWINS, NOBS), ((0, 8), (1, 4)), -0.2, 0.2)), 0.5, 2.0),
        "trajectory": bell_draw(key_list[5], (SUBWINS, LEV, NX, NY), 1.0, 6.0, ((0, 8), (2, 4))),
        "diffusion": jnp.clip(jnp.exp(jax.random.uniform(key_list[6], (LEV,), jnp.float32, math.log(0.05), math.log(0.2))), 0.05, 0.2),
        "drift_rows": jnp.clip(jax.random.uniform(key_list[7], (LEV,), jnp.float32, -0.25, 0.25), -0.25, 0.25),
        "drift_cols": jnp.clip(jax.random.uniform(key_list[8], (LEV,), jnp.float32, -0.25, 0.25), -0.25, 0.25),
        "spread": jnp.clip(jnp.exp(jax.random.uniform(key_list[9], (LEV,), jnp.float32, math.log(0.5), math.log(2.0))), 0.5, 2.0),
        "row_factor": bell_draw(key_list[10], (NX, NX), NX ** -0.5, 0.375, (), jnp.float32),
        "col_factor": bell_draw(key_list[11], (NY, NY), NY ** -0.5, 0.375, (), jnp.float32),
        "layer_in": bell_draw(key_list[12], (HID, LEV), LEV ** -0.5, 0.75),
        "bias_in": bell_draw(key_list[13], (HID,), 1.0, 4.0, (), jnp.float32),
        "layer_out": bell_draw(key_list[14], (LEV, HID), HID ** -0.5, 0.1875),
    }


exact_mode = lax.Precision.HIGHEST


def stencil_step(padded, diffusion, drift_rows, drift_cols, direction):
    centre = padded[:, 1:-1, :]
    row_up = padded[:, 2:, :]
    row_down = padded[:, :-2, :]
    widened = jnp.pad(centre, ((0, 0), (0, 0), (1, 1)))
    col_up = widened[:, :, 2:]
    col_down = widened[:, :, :-2]
    mixing = row_up + row_down + col_up + col_down - 4.0 * centre
    carried = drift_rows * (row_up - row_down) + drift_cols * (col_up - col_down)
    return centre + diffusion * mixing - direction * carried


def bf_round(values):
    return lax.optimization_barrier(values.astype(jnp.bfloat16)).astype(jnp.float32)


def network_both(forward_in, backward_in, trajectory, layer_in, bias_in, layer_out):
    levels, row_count, columns = forward_in.shape
    block_rows = min(row_count, max(1, 1024 // columns))
    weight_in = layer_in.astype(jnp.float32)
    weight_out = layer_out.astype(jnp.float32)

    def select(source, first_row):
        piece = lax.dynamic_slice_in_dim(source, first_row, block_rows, 1)
        return piece.reshape(levels, block_rows * columns)

    def visit(block_index, totals):
        first_row = (block_index * block_rows).astype(jnp.int32)
        path = select(trajectory, first_row).astype(jnp.float32)
        activation = jnp.dot(weight_in, path) + bias_in[:, None]
        gating = jax.nn.sigmoid(activation)
        slopes = gating * (1.0 + activation * (1.0 - gating))
        tangent_in = select(forward_in, first_row)
        hidden = bf_round(slopes * jnp.dot(weight_in, bf_round(tangent_in)))
        tangent_out = tangent_in + jnp.dot(weight_out, hidden)
        adjoint_in = select(backward_in, first_row)
        back_hidden = bf_round(slopes * jnp.dot(weight_out.T, bf_round(adjoint_in)))
        adjoint_out = adjoint_in + jnp.dot(weight_in.T, back_hidden)
        shape = (levels, block_rows, columns)
        return (lax.dynamic_update_slice_in_dim(totals[0], tangent_out.reshape(shape), first_row, 1),
                lax.dynamic_update_slice_in_dim(totals[1], adjoint_out.reshape(shape), first_row, 1))

    empty = jnp.zeros(forward_in.shape, jnp.float32)
    return lax.fori_loop(0, row_count // block_rows, visit, (empty, empty))


def correlate(fields, spread, row_factor, col_factor):
    inner = jnp.einsum('xa,lxy->lay', row_factor, fields, precision=exact_mode)
    inner = jnp.einsum('lay,yb->lab', inner, col_factor, precision=exact_mode)
    outer = jnp.einsum('xa,lab->lxb', row_factor, inner, precision=exact_mode)
    outer = jnp.einsum('lxb,yb->lxy', outer, col_factor, precision=exact_mode)
    return (spread * spread)[:, None, None] * outer


def reference(increment, multiplier, obs_dual, obs_sites, obs_variance, trajectory, diffusion, drift_rows, drift_cols, spread, row_factor, col_factor, layer_in, bias_in, layer_out):
    coefs = (diffusion[:, None, None], drift_rows[:, None, None], drift_cols[:, None, None])

    def stepping(fields, direction):
        for repeat in range(STEPS):
            padded = jnp.pad(fields, ((0, 0), (1, 1), (0, 0)))
            fields = stencil_step(padded, coefs[0], coefs[1], coefs[2], direction)
        return fields

    blank = jnp.zeros((1, LEV, NX, NY), jnp.float32)
    previous = jnp.concatenate([blank, increment[:-1]], 0)

    def per_window(window_items):
        prior_one, mult_one, path_one = window_items
        tangent, adjoint = network_both(stepping(prior_one, 1.0), mult_one, path_one, layer_in, bias_in, layer_out)
        return tangent, stepping(adjoint, -1.0)

    forward, backward = lax.map(per_window, (previous, multiplier, trajectory))
    later = jnp.concatenate([backward[1:], blank], 0)
    correlated = lax.map(lambda fields: correlate(fields, spread, row_factor, col_factor), multiplier)
    state_out = (correlated + increment) - forward

    def observe(fields, positions):
        return fields[positions[0], positions[1], positions[2]]

    seen = jax.vmap(observe)(increment, obs_sites)
    obs_out = obs_variance * obs_dual + seen

    def place(duals, positions):
        return jnp.zeros((LEV, NX, NY), jnp.float32).at[positions[0], positions[1], positions[2]].add(duals)

    placed = jax.vmap(place)(obs_dual, obs_sites)
    mult_out = (multiplier - later) + placed
    return state_out, obs_out, mult_out
```

```python
import functools

import jax
import jax.numpy as jnp
from jax import lax
from jax.experimental import pallas as pl
from jax.experimental.pallas import tpu as pltpu
from jax.sharding import PartitionSpec as P

STEPS = 4
BIAS_TERMS = 3
BIAS_PAD = 16

exact_mode = lax.Precision.HIGHEST
MIB = 2**20


def partner(index, turn, count):
    if count & (count - 1) == 0:
        return index ^ turn
    return lax.rem(turn - index + count, count)


def send(value, turn, shift):
    windows, count = lax.axis_size("win"), lax.axis_size("space")
    pairs = []
    for window in range(max(0, -shift), min(windows, windows - shift)):
        for index in range(count):
            other = index ^ turn if count & (count - 1) == 0 else (turn - index) % count
            pairs.append((window * count + index, (window + shift) * count + other))
    if all(source == target for source, target in pairs):
        return value
    return lax.ppermute(value, ("win", "space"), pairs)


def full_spec(array):
    return pl.BlockSpec(array.shape, lambda *_: (0,) * array.ndim)


def four_steps(field, other, weights, rows, cols):
    keep, row_up, row_down, col_up, col_down = weights
    lane = lax.broadcasted_iota(jnp.int32, (rows, cols), 1)
    source, target = field, other
    result = None
    for step in range(STEPS):
        centre = source[8 : 8 + rows, :]
        up = source[9 : 9 + rows, :]
        down = source[7 : 7 + rows, :]
        right = jnp.where(lane == cols - 1, 0.0, pltpu.roll(centre, cols - 1, 1))
        left = jnp.where(lane == 0, 0.0, pltpu.roll(centre, 1, 1))
        result = keep * centre + row_up * up + row_down * down + col_up * right + col_down * left
        if step < STEPS - 1:
            target[8 : 8 + rows, :] = result
            source, target = target, source
    return result


def clear_edges(rows, cols, *fields):
    for field in fields:
        field[0:8, :] = jnp.zeros((8, cols), jnp.float32)
        field[8 + rows : 16 + rows, :] = jnp.zeros((8, cols), jnp.float32)


def out_kernel(count, rows, cols, place, weights, field, *refs):
    strips, (work, other) = refs[:count], refs[count:]
    level = pl.program_id(0)

    @pl.when(level == 0)
    def _():
        clear_edges(rows, cols, work, other)

    work[8 : 8 + rows, :] = field[0]
    scalars = [weights[term, level] for term in range(5)]
    work[8 : 8 + rows, :] = four_steps(work, other, scalars, rows, cols)
    height = rows // count
    for turn in range(count):
        start = pl.multiple_of(8 + place[turn] * height, 8)
        strips[turn][0] = work[pl.ds(start, height), :]


def stencil_out(field, weights, place):
    levels, rows, cols = field.shape
    count = place.shape[0]
    height = rows // count
    return pl.pallas_call(
        functools.partial(out_kernel, count, rows, cols),
        grid_spec=pltpu.PrefetchScalarGridSpec(
            num_scalar_prefetch=2,
            grid=(levels,),
            in_specs=[pl.BlockSpec((1, rows, cols), lambda level, *_: (level, 0, 0))],
            out_specs=[pl.BlockSpec((1, height, cols), lambda level, *_: (level, 0, 0))] * count,
            scratch_shapes=[pltpu.VMEM((rows + 16, cols), jnp.float32)] * 2,
        ),
        out_shape=[jax.ShapeDtypeStruct((levels, height, cols), jnp.float32)] * count,
        cost_estimate=pl.CostEstimate(
            flops=STEPS * 20 * field.size, bytes_accessed=8 * field.size, transcendentals=0
        ),
        name="stencil_out",
    )(place, weights, field)


def in_kernel(count, rows, cols, place, weights, *refs):
    strips, base, out = refs[:count], refs[count], refs[count + 1]
    work, other = refs[count + 2 :]
    level = pl.program_id(0)

    @pl.when(level == 0)
    def _():
        clear_edges(rows, cols, work, other)

    height = rows // count
    for turn in range(count):
        start = pl.multiple_of(8 + place[turn] * height, 8)
        work[pl.ds(start, height), :] = strips[turn][0]
    scalars = [weights[term, level] for term in range(5)]
    out[0] = base[0] - four_steps(work, other, scalars, rows, cols)


def stencil_in(strips, base, weights, place):
    levels, rows, cols = base.shape
    count = place.shape[0]
    height = rows // count
    strip_spec = pl.BlockSpec((1, height, cols), lambda level, *_: (level, 0, 0))
    slab_spec = pl.BlockSpec((1, rows, cols), lambda level, *_: (level, 0, 0))
    return pl.pallas_call(
        functools.partial(in_kernel, count, rows, cols),
        grid_spec=pltpu.PrefetchScalarGridSpec(
            num_scalar_prefetch=2,
            grid=(levels,),
            in_specs=[strip_spec] * count + [slab_spec],
            out_specs=slab_spec,
            scratch_shapes=[pltpu.VMEM((rows + 16, cols), jnp.float32)] * 2,
        ),
        out_shape=jax.ShapeDtypeStruct(base.shape, jnp.float32),
        cost_estimate=pl.CostEstimate(
            flops=STEPS * 20 * base.size, bytes_accessed=12 * base.size, transcendentals=0
        ),
        name="stencil_in",
    )(place, weights, *strips, base)


def net_kernel(count, levels, rows, cols, *refs):
    strips = refs[:count]
    path, gate, first, second = refs[count : count + 4]
    outs = refs[count + 4 : 2 * count + 4]
    values, paths, results = refs[2 * count + 4 :]
    for turn in range(count):
        span = slice(turn * levels, (turn + 1) * levels)
        values[:, span, :] = jnp.swapaxes(strips[turn][...], 0, 1)
    paths[...] = jnp.swapaxes(path[...].astype(jnp.float32), 0, 1).astype(jnp.bfloat16)
    term = lax.broadcasted_iota(jnp.int32, (BIAS_PAD, cols), 0)
    ones = jnp.where(term < BIAS_TERMS, 1.0, 0.0).astype(jnp.bfloat16)

    def visit(row, carry):
        centre = values[row]
        half = jnp.dot(
            gate[...], jnp.concatenate([paths[row], ones], 0), preferred_element_type=jnp.float32
        )
        hidden = jnp.dot(first[...], centre.astype(jnp.bfloat16), preferred_element_type=jnp.float32)
        bent = jnp.tanh(half)
        slope = (1.0 + bent) * (1.0 + half * (1.0 - bent))
        hidden = (slope * hidden).astype(jnp.bfloat16)
        results[row] = centre + jnp.dot(second[...], hidden, preferred_element_type=jnp.float32)
        return carry

    lax.fori_loop(0, rows, visit, 0, unroll=2)
    for turn in range(count):
        span = slice(turn * levels, (turn + 1) * levels)
        outs[turn][...] = jnp.swapaxes(results[:, span, :], 0, 1)


def network(strips, path, gate, first, second):
    count = len(strips)
    levels, height, cols = strips[0].shape
    rows = min(16, height)
    total = count * levels
    strip_spec = pl.BlockSpec((levels, rows, cols), lambda step: (0, step, 0))
    return pl.pallas_call(
        functools.partial(net_kernel, count, levels, rows, cols),
        grid=(height // rows,),
        in_specs=[strip_spec] * count
        + [pl.BlockSpec((total, rows, cols), lambda step: (0, step, 0))]
        + [full_spec(gate), full_spec(first), full_spec(second)],
        out_specs=[strip_spec] * count,
        out_shape=[jax.ShapeDtypeStruct(strips[0].shape, jnp.float32)] * count,
        scratch_shapes=[
            pltpu.VMEM((rows, total, cols), jnp.float32),
            pltpu.VMEM((rows, total, cols), jnp.bfloat16),
            pltpu.VMEM((rows, total, cols), jnp.float32),
        ],
        compiler_params=pltpu.CompilerParams(vmem_limit_bytes=40 * MIB),
        cost_estimate=pl.CostEstimate(
            flops=4 * 3 * 2 * height * cols * total * first.shape[0],
            bytes_accessed=10 * total * height * cols,
            transcendentals=height * cols * first.shape[0],
        ),
        name="network",
    )(*strips, path, gate, first, second)


def correlate_kernel(spread, row_factor, col_factor, fields, state, out, rows_pair, cols_pair):
    level = pl.program_id(0)
    same = (((1,), (1,)), ((), ()))

    @pl.when(level == 0)
    def _():
        for pair, factor in ((rows_pair, row_factor), (cols_pair, col_factor)):
            pair[...] = lax.dot_general(
                factor[...], factor[...], same, precision=exact_mode,
                preferred_element_type=jnp.float32,
            )

    inner = jnp.dot(
        fields[0], cols_pair[...], precision=exact_mode, preferred_element_type=jnp.float32
    )
    outer = jnp.dot(
        rows_pair[...], inner, precision=exact_mode, preferred_element_type=jnp.float32
    )
    scale = spread[level] * spread[level]
    out[0] = scale * outer + state[0]


def correlate(fields, state, spread, row_factor, col_factor):
    levels, rows, cols = fields.shape
    slab_spec = pl.BlockSpec((1, rows, cols), lambda level, *_: (level, 0, 0))
    return pl.pallas_call(
        correlate_kernel,
        grid_spec=pltpu.PrefetchScalarGridSpec(
            num_scalar_prefetch=1,
            grid=(levels,),
            in_specs=[full_spec(row_factor), full_spec(col_factor), slab_spec, slab_spec],
            out_specs=slab_spec,
            scratch_shapes=[pltpu.VMEM((rows, rows), jnp.float32), pltpu.VMEM((cols, cols), jnp.float32)],
        ),
        out_shape=jax.ShapeDtypeStruct(fields.shape, jnp.float32),
        cost_estimate=pl.CostEstimate(
            flops=6 * 2 * fields.size * (rows + cols), bytes_accessed=12 * fields.size, transcendentals=0
        ),
        name="correlate",
    )(spread, row_factor, col_factor, fields, state)


def combine_kernel(place, whole, strip, out):
    out[...] = whole[...] - strip[...]


def combine(whole, strips, place):
    levels, rows, cols = whole.shape
    count = place.shape[0]
    height = rows // count
    for turn in range(count):
        block = pl.BlockSpec(
            (levels, height, cols), lambda step, place, turn=turn: (0, place[turn], 0)
        )
        strip_spec = pl.BlockSpec((levels, height, cols), lambda step, place: (0, 0, 0))
        whole = pl.pallas_call(
            combine_kernel,
            grid_spec=pltpu.PrefetchScalarGridSpec(
                num_scalar_prefetch=1,
                grid=(1,),
                in_specs=[block, strip_spec],
                out_specs=block,
            ),
            out_shape=jax.ShapeDtypeStruct(whole.shape, jnp.float32),
            input_output_aliases={1: 0},
            cost_estimate=pl.CostEstimate(
                flops=strips[turn].size, bytes_accessed=12 * strips[turn].size, transcendentals=0
            ),
            name="combine",
        )(place, whole, strips[turn])
    return whole


def observe_kernel(group, row_index, col_index, duals, state, mult, base, seen, picked):
    count = picked.shape[0]
    base[...] = mult[...]
    lane = lax.broadcasted_iota(jnp.int32, (1, state.shape[1]), 1)
    spot = lax.broadcasted_iota(jnp.int32, (8, 128), 0) * 128 + lax.broadcasted_iota(
        jnp.int32, (8, 128), 1
    )

    def visit(block, carry):
        for item in range(group):
            index = block * group + item
            row, col = row_index[index], col_index[index]
            found = jnp.where(lane == col, state[pl.ds(row, 1), :], 0.0)
            total = found[:, 0:128]
            for first in range(128, state.shape[1], 128):
                total = total + found[:, first : first + 128]
            picked[pl.ds(index, 1), :] = total
            top = pl.multiple_of((row >> 3) << 3, 8)
            side = pl.multiple_of(jnp.maximum((col >> 7) << 7, 0), 128)
            tile = (pl.ds(top, 8), pl.ds(side, 128))
            hit = spot == jnp.where(col < 0, -1, ((row & 7) << 7) + (col & 127))
            base[tile] = base[tile] + jnp.where(hit, duals[index], 0.0)
        return carry

    lax.fori_loop(0, count // group, visit, 0)
    ones = jnp.ones((8, 128), jnp.float32)
    seen[...] = lax.dot_general(
        ones, picked[...], (((1,), (1,)), ((), ())), precision=exact_mode,
        preferred_element_type=jnp.float32,
    )


def observe(row_index, col_index, duals, state, mult):
    count = duals.shape[0]
    vmem = pl.BlockSpec(memory_space=pltpu.VMEM)
    smem = pl.BlockSpec(memory_space=pltpu.SMEM)
    base, seen = pl.pallas_call(
        functools.partial(observe_kernel, 8),
        in_specs=[smem, smem, smem, vmem, vmem],
        out_specs=[vmem, vmem],
        out_shape=[
            jax.ShapeDtypeStruct(mult.shape, jnp.float32),
            jax.ShapeDtypeStruct((8, count), jnp.float32),
        ],
        scratch_shapes=[pltpu.VMEM((count, 128), jnp.float32)],
        compiler_params=pltpu.CompilerParams(vmem_limit_bytes=40 * MIB),
        cost_estimate=pl.CostEstimate(
            flops=20000 * count, bytes_accessed=12 * mult.size, transcendentals=0
        ),
        name="observe",
    )(row_index, col_index, duals, state, mult)
    return base, seen[0]


def bias_terms(bias):
    terms, rest = [], bias
    for _ in range(BIAS_TERMS):
        term = lax.reduce_precision(rest, 8, 7)
        terms.append(term.astype(jnp.bfloat16))
        rest = rest - term
    zero = jnp.zeros((bias.shape[0], BIAS_PAD - BIAS_TERMS), jnp.bfloat16)
    return jnp.concatenate([jnp.stack(terms, 1), zero], 1)


def body(
    increment,
    multiplier,
    obs_dual,
    obs_sites,
    obs_variance,
    trajectory,
    diffusion,
    drift_rows,
    drift_cols,
    spread,
    row_factor,
    col_factor,
    layer_in,
    bias_in,
    layer_out,
):
    state, mult, path = increment[0], multiplier[0], trajectory[0]
    levels, rows, cols = state.shape
    count = lax.axis_size("space")
    here = lax.axis_index("space")
    height = rows // count
    first_level = here * levels
    turns = range(count)
    place = jnp.stack([partner(here, turn, count) for turn in turns]).astype(jnp.int32)

    def local(values):
        return lax.dynamic_slice_in_dim(values, first_level, levels)

    def weights(direction):
        mix, along, across = local(diffusion), direction * local(drift_rows), direction * local(drift_cols)
        return jnp.stack([1.0 - 4.0 * mix, mix - along, mix + along, mix - across, mix + across])

    mult_strips = [
        send(lax.dynamic_slice_in_dim(mult, place[turn] * height, height, 1), turn, 0) for turn in turns
    ]
    stepped = stencil_out(state, weights(1.0), place)
    state_strips = [send(stepped[turn], turn, 1) for turn in turns]

    half = jnp.asarray(0.5, jnp.bfloat16)
    gate = jnp.concatenate([layer_in, bias_terms(bias_in)], 1) * half
    columns = (place[:, None] * levels + jnp.arange(levels, dtype=jnp.int32)[None, :]).reshape(-1)
    layer_in_own = jnp.take(layer_in, columns, axis=1)
    layer_out_own = jnp.take(layer_out, columns, axis=0)

    partial = correlate(mult, state, local(spread), row_factor, col_factor)

    owned = obs_dual.shape[1]
    positions = obs_sites[0]
    all_duals = [send(obs_dual[0], turn, 0) for turn in turns]
    duals = jnp.concatenate(all_duals)
    ordered = jnp.take(positions.reshape(3, count, owned), place, axis=1).reshape(3, -1)
    local_level = ordered[0] - first_level
    inside = (local_level >= 0) & (local_level < levels)
    row_index = jnp.where(inside, local_level * rows + ordered[1], 0)
    col_index = jnp.where(inside, ordered[2], -1)
    base, seen = observe(
        row_index, col_index, duals, state.reshape(-1, cols), mult.reshape(-1, cols)
    )
    base = base.reshape(mult.shape)
    parts = [send(seen[turn * owned : (turn + 1) * owned], turn, 0) for turn in turns]
    obs_out = obs_variance[0] * obs_dual[0] + sum(parts[1:], parts[0])

    adjoint = network(mult_strips, path, gate, layer_out_own.T, layer_in_own.T * half)
    adjoint_strips = [send(adjoint[turn], turn, -1) for turn in turns]
    tangent = network(state_strips, path, gate, layer_in_own, layer_out_own * half)
    tangent_strips = [send(tangent[turn], turn, 0) for turn in turns]

    state_out = combine(partial, tangent_strips, place)
    mult_out = stencil_in(adjoint_strips, base, weights(-1.0), place)
    return (state_out[None], obs_out[None], mult_out[None])


def solution(mesh):
    placed = (
        P("win", "space", None, None),
        P("win", "space", None, None),
        P("win", "space"),
        P("win", None, None),
        P("win", "space"),
        P("win", None, "space", None),
        P(),
        P(),
        P(),
        P(),
        P(),
        P(),
        P(),
        P(),
        P(),
    )
    return jax.shard_map(
        body,
        mesh=mesh,
        in_specs=placed,
        out_specs=(P("win", "space", None, None), P("win", "space"), P("win", "space", None, None)),
        check_vma=False,
    )
```

```python
import functools

import jax
import jax.numpy as jnp
from jax import lax
from jax.experimental import pallas as pl
from jax.experimental.pallas import tpu as pltpu
from jax.sharding import PartitionSpec as P

STEPS = 4
BIAS_TERMS = 3
BIAS_PAD = 16
PAIR = 2
GROUP = 8
LANES = 128
BLOCK = 128

exact_mode = lax.Precision.HIGHEST
MIB = 2**20
ROOM = 56 * MIB
COST = pl.CostEstimate(flops=10**6, bytes_accessed=10**5, transcendentals=0)
LONG = pl.CostEstimate(flops=10**12, bytes_accessed=10**9, transcendentals=0)


def send(value, shift, turn, swap):
    windows, count = lax.axis_size("win"), lax.axis_size("space")
    pairs = []
    for window in range(max(0, -shift), min(windows, windows - shift)):
        for index in range(count):
            other = meet(index // PAIR, turn, count // PAIR) * PAIR + (index % PAIR ^ swap)
            pairs.append((window * count + index, (window + shift) * count + other))
    if all(source == target for source, target in pairs):
        return value
    return lax.ppermute(value, ("win", "space"), pairs)


def meet(group, turn, groups):
    if groups & (groups - 1) == 0:
        return group ^ turn
    return (turn - group + groups) % groups


def ignoring(kernel, first, number):
    def run(*refs):
        kernel(*refs[:first], *refs[first + number :])

    return run


def later(value, *earlier, cost=None):
    return pl.pallas_call(
        lambda *refs: None,
        in_specs=[pl.BlockSpec(memory_space=pl.ANY)] * (1 + len(earlier)),
        out_specs=pl.BlockSpec(memory_space=pl.ANY),
        out_shape=jax.ShapeDtypeStruct(value.shape, value.dtype),
        input_output_aliases={0: 0},
        cost_estimate=COST if cost is None else cost,
        name="later",
    )(value, *earlier)


def full_spec(array):
    return pl.BlockSpec(array.shape, lambda *_: (0,) * array.ndim)


def parts_of(row):
    cols = row.shape[-1]
    return tuple(row[..., first : first + LANES] for first in range(0, cols, LANES))


def step_row(rows, weights):
    below, centre, above = rows
    width = centre[0].shape[-1]
    lane = lax.broadcasted_iota(jnp.int32, centre[0].shape, 1)
    first, last = lane == 0, lane == width - 1
    lefts = [pltpu.roll(part, 1, 1) for part in centre]
    rights = [pltpu.roll(part, width - 1, 1) for part in centre]
    results = []
    for at, part in enumerate(centre):
        keep, row_up, row_down, col_up, col_down = weights
        left = jnp.where(first, lefts[at - 1] if at else 0.0, lefts[at])
        right = jnp.where(last, rights[at + 1] if at + 1 < len(centre) else 0.0, rights[at])
        sides = col_up * right + col_down * left
        results.append((keep * part + sides) + (row_up * above[at] + row_down * below[at]))
    return tuple(results)


def all_steps(source, target, weights, rows):
    cols = source.shape[-1]
    for field in (source, target):
        for edge in (0, rows + 1):
            field[edge] = jnp.zeros(field.shape[1:], jnp.float32)
    block = min(BLOCK, rows)
    for _ in range(STEPS):

        def visit(number, carry, source=source, target=target):
            first = number * block
            for row in range(block):
                below, centre, above = (parts_of(source[first + row + at]) for at in range(3))
                for at, part in enumerate(step_row((below, centre, above), weights)):
                    target[first + row + 1, :, at * LANES : at * LANES + part.shape[-1]] = part
            return carry

        lax.fori_loop(0, rows // block, visit, 0)
        source, target = target, source
    return source


def out_kernel(count, place, weights, field, *refs):
    strips, (work, other) = refs[:count], refs[count:]
    rows = field.shape[1]

    def turn(number, carry):
        first = pl.multiple_of(number * GROUP, GROUP)
        work[pl.ds(first + 1, GROUP)] = jnp.swapaxes(field[:, pl.ds(first, GROUP), :], 0, 1)
        return carry

    lax.fori_loop(0, rows // GROUP, turn, 0, unroll=4)
    done = all_steps(work, other, [weights[term] for term in range(5)], rows)
    for number, strip in enumerate(strips):
        strip[...] = done[pl.ds(place[number] + 1, strip.shape[0])]


def weight_spec(depth):
    return pl.BlockSpec((5, depth, LANES), lambda step, *_: (0, step, 0))


def stencil_out(field, weights, starts, heights, after):
    levels, rows, cols = field.shape
    depth = min(8, levels)
    return pl.pallas_call(
        ignoring(functools.partial(out_kernel, len(heights)), 3, len(after)),
        grid_spec=pltpu.PrefetchScalarGridSpec(
            num_scalar_prefetch=1,
            grid=(levels // depth,),
            in_specs=[
                weight_spec(depth),
                pl.BlockSpec((depth, rows, cols), lambda step, *_: (step, 0, 0)),
            ]
            + [pl.BlockSpec(memory_space=pl.ANY)] * len(after),
            out_specs=[
                pl.BlockSpec((height, depth, cols), lambda step, *_: (0, step, 0))
                for height in heights
            ],
            scratch_shapes=[pltpu.VMEM((rows + 2, depth, cols), jnp.float32)] * 2,
        ),
        out_shape=[jax.ShapeDtypeStruct((height, levels, cols), jnp.float32) for height in heights],
        compiler_params=pltpu.CompilerParams(vmem_limit_bytes=ROOM),
        cost_estimate=LONG,
        name="stencil_out",
    )(starts, weights, field, *after)


def in_kernel(count, height, place, core, weights, *refs):
    strips, base, results = refs[:count], refs[count], refs[count + 1 : 2 * count + 1]
    whole, out, state_out, work, other = refs[2 * count + 1 :]
    rows = out.shape[1]
    for turn in range(count):
        work[pl.ds(place[turn] * height + 1, height)] = strips[turn][...]
    done = all_steps(work, other, [weights[term] for term in range(5)], rows)

    def finish(group, carry):
        first = pl.multiple_of(group * GROUP, GROUP)
        span = (slice(None), pl.ds(first, GROUP), slice(None))
        out[span] = base[span] - jnp.swapaxes(done[pl.ds(first + 1, GROUP)], 0, 1)
        return carry

    lax.fori_loop(0, rows // GROUP, finish, 0, unroll=4)
    for turn in range(count):
        span = pl.ds(pl.multiple_of(place[turn] * height, 8), height)
        state_out[:, span, :] = whole[:, span, :] - results[turn][...]


def finish_both(strips, base, results, whole, weights, place, core):
    levels, rows, cols = base.shape
    count = place.shape[0]
    height = rows // count
    depth = min(8, levels)
    steps = levels // depth
    far = pl.BlockSpec((height, depth, cols), lambda step, *_: (0, step, 0))
    if levels % 8:
        strips = [
            lax.dynamic_slice_in_dim(strip, core[0] * levels, levels, 1)
            if strip.shape[1] != levels
            else strip
            for strip in strips
        ]
        near = far
    else:
        near = pl.BlockSpec(
            (height, depth, cols), lambda step, place, core: (0, core[0] * steps + step, 0)
        )
    slab_spec = pl.BlockSpec((depth, rows, cols), lambda step, *_: (step, 0, 0))
    result_spec = pl.BlockSpec((depth, height, cols), lambda step, *_: (step, 0, 0))
    return pl.pallas_call(
        functools.partial(in_kernel, count, height),
        grid_spec=pltpu.PrefetchScalarGridSpec(
            num_scalar_prefetch=2,
            grid=(steps,),
            in_specs=[weight_spec(depth)]
            + [far if strip.shape[1] == levels else near for strip in strips]
            + [slab_spec]
            + [result_spec] * count
            + [slab_spec],
            out_specs=[slab_spec, slab_spec],
            scratch_shapes=[pltpu.VMEM((rows + 2, depth, cols), jnp.float32)] * 2,
        ),
        out_shape=[jax.ShapeDtypeStruct(base.shape, jnp.float32)] * 2,
        compiler_params=pltpu.CompilerParams(vmem_limit_bytes=ROOM),
        cost_estimate=COST,
        name="finish_both",
    )(place, core, weights, *strips, base, *results, whole)


def net_kernel(groups, levels, rows, cols, rows_in, at, core, *refs):
    count = groups * PAIR
    strips = refs[:count]
    path, gate, first, second = refs[count : count + 4]
    outs, (values, paths, results) = refs[count + 4 : -3], refs[-3:]
    for side in range(PAIR):

        @pl.when(core[0] == side)
        def _():
            for turn in range(count):
                start = (turn // PAIR) * PAIR * levels + (side ^ (turn % PAIR)) * levels
                strip = strips[turn][...]
                strip = strip if rows_in else jnp.swapaxes(strip, 0, 1)
                values[:, start : start + levels, :] = strip

    paths[...] = jnp.swapaxes(path[...].astype(jnp.float32), 0, 1).astype(jnp.bfloat16)
    term = lax.broadcasted_iota(jnp.int32, (BIAS_PAD, cols), 0)
    ones = jnp.where(term < BIAS_TERMS, 1.0, 0.0).astype(jnp.bfloat16)

    def visit(row, carry):
        centre = values[row]
        half = jnp.dot(
            gate[...], jnp.concatenate([paths[row], ones], 0), preferred_element_type=jnp.float32
        )
        hidden = jnp.dot(first[...], centre.astype(jnp.bfloat16), preferred_element_type=jnp.float32)
        bent = jnp.tanh(half)
        slope = (1.0 + bent) * (1.0 + half * (1.0 - bent))
        hidden = (slope * hidden).astype(jnp.bfloat16)
        results[row] = centre + jnp.dot(second[...], hidden, preferred_element_type=jnp.float32)
        return carry

    lax.fori_loop(0, rows, visit, 0, unroll=2)
    def put(out, start, depth):
        result = results[:, start : start + depth, :]
        out[...] = jnp.swapaxes(result, 0, 1) if rows_in else result

    if rows_in:
        for side in range(PAIR):

            @pl.when(core[0] == side)
            def _():
                for turn in range(count):
                    put(outs[turn], (turn // PAIR * PAIR + (side ^ (turn % PAIR))) * levels, levels)

    else:
        for group in range(groups):
            put(outs[group], group * PAIR * levels, PAIR * levels)


def network(strips, offsets, core, path, gate, first, second, after, rows_in):
    count = len(strips)
    groups = count // PAIR
    total, height, cols = path.shape
    levels = total // count
    rows = min(16, height)
    if rows_in:
        out_specs = [pl.BlockSpec((levels, rows, cols), lambda step, *_: (0, step, 0))] * count
        out_shapes = [(levels, height, cols)] * count
    else:
        depth = PAIR * levels
        out_specs = [pl.BlockSpec((rows, depth, cols), lambda step, *_: (step, 0, 0))] * groups
        out_shapes = [(height, depth, cols)] * groups
    in_specs = []
    for turn in range(count):
        if rows_in:
            spec = pl.BlockSpec(
                (rows, levels, cols), lambda step, at, core, turn=turn: (at[turn] + step, 0, 0)
            )
        else:
            spec = pl.BlockSpec(
                (levels, rows, cols), lambda step, at, core, turn=turn: (0, at[turn] + step, 0)
            )
        in_specs.append(spec)
    return pl.pallas_call(
        ignoring(functools.partial(net_kernel, groups, levels, rows, cols, rows_in), count + 6, len(after)),
        grid_spec=pltpu.PrefetchScalarGridSpec(
            num_scalar_prefetch=2,
            grid=(height // rows,),
            in_specs=in_specs
            + [pl.BlockSpec((total, rows, cols), lambda step, *_: (0, step, 0))]
            + [full_spec(gate), full_spec(first), full_spec(second)]
            + [pl.BlockSpec(memory_space=pl.ANY)] * len(after),
            out_specs=out_specs,
            scratch_shapes=[
                pltpu.VMEM((rows, total, cols), jnp.float32),
                pltpu.VMEM((rows, total, cols), jnp.bfloat16),
                pltpu.VMEM((rows, total, cols), jnp.float32),
            ],
        ),
        out_shape=[jax.ShapeDtypeStruct(shape, jnp.float32) for shape in out_shapes],
        compiler_params=pltpu.CompilerParams(vmem_limit_bytes=ROOM),
        cost_estimate=COST if rows_in else LONG,
        name="network",
    )(offsets // rows, core, *strips, path, gate, first, second, *after)


def halves(value):
    high = value.astype(jnp.bfloat16)
    return high, (value - high.astype(jnp.float32)).astype(jnp.bfloat16)


def correlate_kernel(depth, spread, row_factor, col_factor, fields, state, out, left, right):
    step = pl.program_id(0)
    same = (((1,), (1,)), ((), ()))

    @pl.when(step == 0)
    def _():
        pairs = [
            lax.dot_general(
                factor[...], factor[...], same, precision=exact_mode,
                preferred_element_type=jnp.float32,
            )
            for factor in (row_factor, col_factor)
        ]
        high, low = halves(pairs[0])
        left[...] = jnp.concatenate([high, low, high], 1)
        high, low = halves(pairs[1])
        right[...] = jnp.concatenate([high, low, high], 0)

    rows, cols = fields.shape[1:]
    high, low = halves(fields[...].reshape(depth * rows, cols))
    inner = jnp.dot(
        jnp.concatenate([high, high, low], 1), right[...], preferred_element_type=jnp.float32
    )
    high, low = halves(inner)
    for item in range(depth):
        span = slice(item * rows, (item + 1) * rows)
        outer = jnp.dot(
            left[...],
            jnp.concatenate([high[span], high[span], low[span]], 0),
            preferred_element_type=jnp.float32,
        )
        scale = spread[step * depth + item] * spread[step * depth + item]
        out[item] = scale * outer + state[item]


def correlate(fields, state, spread, row_factor, col_factor, after):
    levels, rows, cols = fields.shape
    depth = min(4, levels)
    slab_spec = pl.BlockSpec((depth, rows, cols), lambda step, *_: (step, 0, 0))
    return pl.pallas_call(
        ignoring(functools.partial(correlate_kernel, depth), 5, len(after)),
        grid_spec=pltpu.PrefetchScalarGridSpec(
            num_scalar_prefetch=1,
            grid=(levels // depth,),
            in_specs=[full_spec(row_factor), full_spec(col_factor), slab_spec, slab_spec]
            + [pl.BlockSpec(memory_space=pl.ANY)] * len(after),
            out_specs=slab_spec,
            scratch_shapes=[
                pltpu.VMEM((rows, 3 * rows), jnp.bfloat16),
                pltpu.VMEM((3 * cols, cols), jnp.bfloat16),
            ],
        ),
        out_shape=jax.ShapeDtypeStruct(fields.shape, jnp.float32),
        compiler_params=pltpu.CompilerParams(vmem_limit_bytes=ROOM),
        cost_estimate=LONG,
        name="correlate",
    )(spread, row_factor, col_factor, fields, state, *after)


def observe_kernel(group, row_index, col_index, duals, state, mult, base, seen, picked, found):
    count = picked.shape[0]
    base[...] = mult[...]
    picked[...] = jnp.zeros_like(picked)
    lane = lax.broadcasted_iota(jnp.int32, (1, state.shape[1]), 1)
    spot = lax.broadcasted_iota(jnp.int32, (8, 128), 0) * 128 + lax.broadcasted_iota(
        jnp.int32, (8, 128), 1
    )

    def collect(block, number):
        for item in range(group):
            index = block * group + item
            found[number] = index
            number = number + jnp.where(col_index[index] >= 0, 1, 0)
        return number

    number = lax.fori_loop(0, count // group - 1, collect, 0)
    for item in range(group):
        found[number + item] = count - group

    def visit(block, carry):
        for item in range(group):
            index = found[block * group + item]
            row, col = row_index[index], col_index[index]
            here = jnp.where(lane == col, state[pl.ds(row, 1), :], 0.0)
            total = here[:, 0:128]
            for first in range(128, state.shape[1], 128):
                total = total + here[:, first : first + 128]
            picked[pl.ds(index, 1), :] = total
            top = pl.multiple_of((row >> 3) << 3, 8)
            side = pl.multiple_of(jnp.maximum((col >> 7) << 7, 0), 128)
            tile = (pl.ds(top, 8), pl.ds(side, 128))
            hit = spot == jnp.where(col < 0, -1, ((row & 7) << 7) + (col & 127))
            base[tile] = base[tile] + jnp.where(hit, duals[index], 0.0)
        return carry

    lax.fori_loop(0, (number + group - 1) // group, visit, 0)
    ones = jnp.ones((8, 128), jnp.float32)
    seen[...] = lax.dot_general(
        ones, picked[...], (((1,), (1,)), ((), ())), precision=exact_mode,
        preferred_element_type=jnp.float32,
    )


def observe(row_index, col_index, duals, state, mult, after):
    count = duals.shape[0]
    row_index = jnp.pad(row_index, (0, GROUP))
    col_index = jnp.pad(col_index, (0, GROUP), constant_values=-1)
    duals = jnp.pad(duals, (0, GROUP))
    vmem = pl.BlockSpec(memory_space=pltpu.VMEM)
    smem = pl.BlockSpec(memory_space=pltpu.SMEM)
    base, seen = pl.pallas_call(
        ignoring(functools.partial(observe_kernel, GROUP), 5, len(after)),
        in_specs=[smem, smem, smem, vmem, vmem] + [pl.BlockSpec(memory_space=pl.ANY)] * len(after),
        out_specs=[vmem, vmem],
        out_shape=[
            jax.ShapeDtypeStruct(mult.shape, jnp.float32),
            jax.ShapeDtypeStruct((8, count + GROUP), jnp.float32),
        ],
        scratch_shapes=[
            pltpu.VMEM((count + GROUP, 128), jnp.float32),
            pltpu.SMEM((count + 2 * GROUP,), jnp.int32),
        ],
        compiler_params=pltpu.CompilerParams(vmem_limit_bytes=ROOM),
        cost_estimate=LONG,
        name="observe",
    )(row_index, col_index, duals, state, mult, *after)
    return base, seen[0, :count]


def bias_terms(bias):
    terms, rest = [], bias
    for _ in range(BIAS_TERMS):
        term = lax.reduce_precision(rest, 8, 7)
        terms.append(term.astype(jnp.bfloat16))
        rest = rest - term
    zero = jnp.zeros((bias.shape[0], BIAS_PAD - BIAS_TERMS), jnp.bfloat16)
    return jnp.concatenate([jnp.stack(terms, 1), zero], 1)


def body(
    increment,
    multiplier,
    obs_dual,
    obs_sites,
    obs_variance,
    trajectory,
    diffusion,
    drift_rows,
    drift_cols,
    spread,
    row_factor,
    col_factor,
    layer_in,
    bias_in,
    layer_out,
):
    state, mult, path = increment[0], multiplier[0], trajectory[0]
    levels, rows, cols = state.shape
    count = lax.axis_size("space")
    groups = count // PAIR
    here = lax.axis_index("space")
    group, core = here // PAIR, here % PAIR
    height = rows // count
    pair_rows = PAIR * height
    first_level = here * levels
    turns = range(groups)
    group_place = jnp.stack([meet(group, turn, groups) for turn in turns]).astype(jnp.int32)
    place = (group_place[:, None] * PAIR + (core ^ jnp.arange(PAIR))[None, :]).reshape(-1)
    place = place.astype(jnp.int32)
    core_ref = core.astype(jnp.int32)[None]

    def local(values):
        return lax.dynamic_slice_in_dim(values, first_level, levels)

    def weights(direction):
        mix, along, across = local(diffusion), direction * local(drift_rows), direction * local(drift_cols)
        terms = jnp.stack([1.0 - 4.0 * mix, mix - along, mix + along, mix - across, mix + across])
        return jnp.broadcast_to(terms[:, :, None], (5, levels, LANES))

    def swap(value, size, axis):
        return send(lax.dynamic_slice_in_dim(value, (1 - core) * size, size, axis), 0, 0, 1)

    all_duals = [send(obs_dual[0], 0, turn, side) for turn in turns for side in range(PAIR)]

    starts = jnp.stack([here * height, (here ^ 1) * height] + [group_place[turn] * pair_rows for turn in turns[1:]])
    stepped = stencil_out(
        state, weights(1.0), starts.astype(jnp.int32), [height] * PAIR + [pair_rows] * (groups - 1),
        all_duals[1:],
    )
    arrived = [send(stepped[0], 1, 0, 0), send(stepped[1], 1, 0, 1)]
    crossing = [
        send(lax.dynamic_slice_in_dim(mult, group_place[turn] * pair_rows, pair_rows, 1), 0, turn, 0)
        for turn in turns[1:]
    ]

    half = jnp.asarray(0.5, jnp.bfloat16)
    gate = jnp.concatenate([layer_in, bias_terms(bias_in)], 1) * half
    order = (
        group_place[:, None] * (PAIR * levels) + jnp.arange(PAIR * levels, dtype=jnp.int32)[None, :]
    ).reshape(-1)
    layer_in_own = jnp.take(layer_in, order, axis=1)
    layer_out_own = jnp.take(layer_out, order, axis=0)

    other_start = later(place, stepped[0])[1] * height
    own_swapped = send(lax.dynamic_slice_in_dim(mult, other_start, height, 1), 0, 0, 1)
    owned = obs_dual.shape[1]
    positions = obs_sites[0]
    duals = jnp.concatenate(all_duals)
    ordered = jnp.take(positions.reshape(3, count, owned), place, axis=1).reshape(3, -1)
    local_level = ordered[0] - first_level
    inside = (local_level >= 0) & (local_level < levels)
    row_index = jnp.where(inside, local_level * rows + ordered[1], 0)
    col_index = jnp.where(inside, ordered[2], -1)
    base, seen = observe(
        row_index, col_index, duals, state.reshape(-1, cols), mult.reshape(-1, cols),
        [stepped[0], own_swapped],
    )
    base = base.reshape(mult.shape)
    seen = seen.reshape(groups, PAIR, owned)
    seen = seen[:, 0] + send(seen[:, 1], 0, 0, 1)
    parts = [send(seen[turn], 0, turn, 0) for turn in turns]
    obs_out = obs_variance[0] * obs_dual[0] + sum(parts[1:], parts[0])
    partial = correlate(mult, state, local(spread), row_factor, col_factor, [base, *arrived[:PAIR]])

    crossing = [later(value, partial, base) for value in crossing]
    for turn in turns[1:]:
        arrived.append(send(later(stepped[turn + 1], *arrived[:PAIR], base), 1, turn, 0))

    zero = jnp.int32(0)
    mult_strips = [mult, own_swapped]
    offsets = [here * height, zero]
    for value in crossing:
        mult_strips += [value, swap(value, height, 1)]
        offsets += [core * height, zero]
    adjoint = network(
        mult_strips, jnp.stack(offsets).astype(jnp.int32), core_ref, path, gate,
        layer_out_own.T, layer_in_own.T * half, [partial, obs_out], False,
    )
    ready = adjoint[0]
    adjoint = [send(adjoint[0], -1, 0, 0)] + [send(adjoint[turn], 0, turn, 0) for turn in turns[1:]]
    state_strips, offsets = arrived[:PAIR], [zero, zero]
    for value in arrived[PAIR:]:
        value = later(value, ready, cost=LONG)
        state_strips += [value, swap(value, height, 0)]
        offsets += [core * height, zero]
    tangent = network(
        state_strips, jnp.stack(offsets).astype(jnp.int32), core_ref, path, gate,
        layer_in_own, layer_out_own * half, [ready], True,
    )
    done = tangent[0]
    tangent = [send(tangent[PAIR * turn + side], 0, turn, side) for turn in turns for side in range(PAIR)]
    adjoint = adjoint[:1] + [send(later(value, done, cost=LONG), -1, 0, 0) for value in adjoint[1:]]
    adjoint_strips = []
    for value in adjoint:
        value = later(value, done, cost=LONG)
        adjoint_strips += [value, swap(value, levels, 1)]
    mult_out, state_out = finish_both(
        adjoint_strips, base, tangent, partial, weights(-1.0), place, core_ref
    )
    return (state_out[None], obs_out[None], mult_out[None])


def solution(mesh):
    placed = (
        P("win", "space", None, None),
        P("win", "space", None, None),
        P("win", "space"),
        P("win", None, None),
        P("win", "space"),
        P("win", None, "space", None),
        P(),
        P(),
        P(),
        P(),
        P(),
        P(),
        P(),
        P(),
        P(),
    )
    return jax.shard_map(
        body,
        mesh=mesh,
        in_specs=placed,
        out_specs=(P("win", "space", None, None), P("win", "space"), P("win", "space", None, None)),
        check_vma=False,
    )
```
